32 devices in a mesh: parts: 2 (over y), tensor: 4 (over z), dp: 4 (over x, core).
Axes of the slice: x: 2, y: 2, z: 4, core: 2. Of those that a mesh axis runs over, the one named last changes fastest.
Arguments:
- inputs_x: bfloat16 [8192, 4096], P(('parts', 'dp'), 'tensor'), parts along dimension 0, may hold values from -6 to 6
- hidden: bfloat16 [8192, 14336], P(('parts', 'dp'), 'tensor'), parts along dimension 0, may hold values from -6 to 6
- grad_gate: bfloat16 [8192, 14336], P(('parts', 'dp'), 'tensor'), parts along dimension 0, may hold values from -6 to 6
- grad_up: bfloat16 [8192, 14336], P(('parts', 'dp'), 'tensor'), parts along dimension 0, may hold values from -6 to 6
- grad_down: bfloat16 [8192, 4096], P(('parts', 'dp'), 'tensor'), parts along dimension 0, may hold values from -6 to 6
- proj_x: bfloat16 [4096, 128], P('tensor'), may hold values from -0.09375 to 0.09375
- proj_hidden: bfloat16 [14336, 64], P('tensor'), may hold values from -0.046875 to 0.046875
- proj_gate: bfloat16 [14336, 64], P('tensor'), may hold values from -0.046875 to 0.046875
- proj_up: bfloat16 [14336, 64], P('tensor'), may hold values from -0.046875 to 0.046875
- proj_down: bfloat16 [4096, 64], P('tensor'), may hold values from -0.09375 to 0.09375
- queries: bfloat16 [4096, 3, 4096], P('dp', None, 'tensor'), may hold values from -0.078125 to 0.078125
Outputs:
- scores: float32 [16, 4096], P(('parts', 'dp'), 'tensor'), parts along dimension 0
The draws below stay inside these ranges and needn't reach their ends.
There are 2 independent parts, one for each index of `parts`. The reference program is written for one: setup_inputs(seed, part) draws one part's arguments, and reference() takes and returns one part's arrays. A program takes and returns all parts, laid end to end along the dimension named above; an argument that names none is the same for every part. Nothing has to cross between parts.
All inputs are finite; a program needn't handle non-finite values.
Results may differ from the reference program's by a relative error of at most 0.0003.
Values may be sent and summed in bfloat16 or wider, within the bound.
A program may use at most 128 MiB of HBM per device.

```python
import jax
import jax.numpy as jnp
from jax import lax

D = 4096
FF = 14336
PROJ = 64
LEN = 512
QUERIES = 4096
TOKENS = 4096


def with_spikes(result, rng, source, target, parts, factor):
    def block_of(dim):
        return (jnp.arange(result.shape[dim]) // (result.shape[dim] // parts)).reshape((-1,) + (1,) * (result.ndim - 1 - dim))

    near = jax.random.permutation(rng, parts)[block_of(target)]
    far = (block_of(target) + parts // 2) % parts
    return jnp.where((block_of(source) == near) | (block_of(source) == far), factor * result, result)


def levels(key, shape, pieces, least, largest):
    level = 1.0
    for position, shards_of in pieces:
        steps = jax.random.uniform(jax.random.fold_in(jax.random.fold_in(key, 6), position), (shards_of,), jnp.float32, least / len(pieces), largest / len(pieces))
        level = level * jnp.repeat(jnp.exp(steps), shape[position] // shards_of).reshape((-1,) + (1,) * (len(shape) - 1 - position))
    return level


def centred(stream_key, dims, deviation, bound, shards=(), dtype=jnp.bfloat16):
    entries = deviation * jax.random.normal(stream_key, dims, jnp.float32)
    if shards:
        entries = entries * levels(stream_key, dims, shards, -0.22, 0.18)
    return jnp.clip(entries, -bound, bound).astype(dtype)


def bell_draw_with(key, shape, scale, most, pieces, heavy, kind=jnp.bfloat16):
    drawn = scale * jax.random.normal(key, shape, jnp.float32)
    if pieces:
        drawn = drawn * levels(key, shape, pieces, -0.22, 0.18)
    return jnp.clip(with_spikes(drawn, jax.random.fold_in(key, 3), *heavy), -most, most).astype(kind)


def setup_inputs(seed: int = 0, part: int = 0) -> dict:
    streams_of = jax.random.split(jax.random.key(seed), 12)
    part_splits = jax.random.split(jax.random.fold_in(streams_of[11], part), 12)
    return {
        "inputs_x": centred(part_splits[0], (TOKENS, D), 1.0, 6.0, ((0, 4), (1, 4))),
        "hidden": centred(part_splits[1], (TOKENS, FF), 1.0, 6.0, ((0, 4), (1, 4))),
        "grad_gate": centred(part_splits[2], (TOKENS, FF), 1.0, 6.0, ((0, 4), (1, 4))),
        "grad_up": centred(part_splits[3], (TOKENS, FF), 1.0, 6.0, ((0, 4), (1, 4))),
        "grad_down": centred(part_splits[4], (TOKENS, D), 1.0, 6.0, ((0, 4), (1, 4))),
        "proj_x": centred(streams_of[5], (D, 2 * PROJ), D ** -0.5, 0.09375, ((0, 4),)),
        "proj_hidden": centred(streams_of[6], (FF, PROJ), FF ** -0.5, 0.046875, ((0, 4),)),
        "proj_gate": centred(streams_of[7], (FF, PROJ), FF ** -0.5, 0.046875, ((0, 4),)),
        "proj_up": centred(streams_of[8], (FF, PROJ), FF ** -0.5, 0.046875, ((0, 4),)),
        "proj_down": centred(streams_of[9], (D, PROJ), D ** -0.5, 0.09375, ((0, 4),)),
        "queries": bell_draw_with(streams_of[10], (QUERIES, 3, PROJ * PROJ), (3 * PROJ * PROJ) ** -0.5, 0.078125, ((0, 4), (2, 4)), (2, 0, 4, 2.0)),
    }


def project(values, factors):
    return jnp.dot(values, factors, preferred_element_type=jnp.float32)


def reference(inputs_x, hidden, grad_gate, grad_up, grad_down, proj_x, proj_hidden, proj_gate, proj_up, proj_down, queries):
    proj_inputs = project(inputs_x, proj_x)
    proj_hiddens = project(hidden, proj_hidden)
    inputs_all = jnp.stack([proj_inputs[:, :PROJ], proj_inputs[:, PROJ:], proj_hiddens], 1)
    outputs_all = jnp.stack([project(grad_gate, proj_gate), project(grad_up, proj_up), project(grad_down, proj_down)], 1)
    example_count = inputs_all.shape[0] // LEN
    inputs_all = inputs_all.reshape(example_count, LEN, 3, PROJ)
    outputs_all = outputs_all.reshape(example_count, LEN, 3, PROJ)
    gradients = jnp.einsum('elmi,elmj->emij', outputs_all, inputs_all, precision=lax.Precision.HIGHEST)
    gradients = (gradients * (LEN ** -0.5)).reshape(example_count, 3, PROJ * PROJ)
    return jnp.einsum('emv,qmv->eq', gradients, queries.astype(jnp.float32), precision=lax.Precision.HIGHEST)
```

```python
import jax
import jax.numpy as jnp
from jax import lax
from jax.sharding import PartitionSpec as P

LEN = 512


def project(values, factors):
    return jnp.dot(values, factors, preferred_element_type=jnp.float32)


def shards(
    inputs_x,
    hidden,
    grad_gate,
    grad_up,
    grad_down,
    proj_x,
    proj_hidden,
    proj_gate,
    proj_up,
    proj_down,
    queries,
):
    local_terms = jnp.concatenate(
        [
            project(inputs_x, proj_x),
            project(hidden, proj_hidden),
            project(grad_gate, proj_gate),
            project(grad_up, proj_up),
            project(grad_down, proj_down),
        ],
        1,
    )
    width = proj_hidden.shape[1]
    devices = lax.axis_size("tensor")
    groups = lax.axis_size("dp")
    examples = local_terms.shape[0] // LEN
    factor = LEN ** (-0.5)
    summed = lax.psum_scatter(
        local_terms.reshape(examples, devices, LEN // devices, 6 * width),
        "tensor",
        scatter_dimension=1,
        tiled=True,
    )
    summed = summed.reshape(examples, LEN // devices, 2, 3, width)
    gradients = jnp.einsum(
        "elmi,elmj->emij", summed[:, :, 1], summed[:, :, 0], precision=lax.Precision.HIGHEST
    )
    gradients = lax.psum_scatter(gradients * factor, "tensor", scatter_dimension=2, tiled=True)
    gradients = gradients.reshape(examples, 3, width // devices * width)
    gradients = lax.all_gather(gradients, "dp", axis=0, tiled=True)
    high = lax.reduce_precision(gradients, 8, 7)
    low = gradients - high
    both = jnp.concatenate([high, low], 0).astype(jnp.bfloat16)
    terms = jnp.einsum("emv,qmv->eq", both, queries, preferred_element_type=jnp.float32)
    terms = terms[: examples * groups] + terms[examples * groups :]
    scores = lax.psum(terms, "tensor")
    scores = lax.all_to_all(scores, "dp", split_axis=0, concat_axis=1, tiled=True)
    columns = scores.shape[1] // devices
    return lax.dynamic_slice_in_dim(scores, lax.axis_index("tensor") * columns, columns, 1)


def solution(mesh):
    placed = (
        P(("parts", "dp"), "tensor"),
        P(("parts", "dp"), "tensor"),
        P(("parts", "dp"), "tensor"),
        P(("parts", "dp"), "tensor"),
        P(("parts", "dp"), "tensor"),
        P("tensor", None),
        P("tensor", None),
        P("tensor", None),
        P("tensor", None),
        P("tensor", None),
        P("dp", None, "tensor"),
    )
    return jax.shard_map(
        shards, mesh=mesh, in_specs=placed, out_specs=P(("parts", "dp"), "tensor"), check_vma=False
    )
```

```python
import functools

import jax
import jax.numpy as jnp
from jax import lax
from jax.experimental import pallas as pl
from jax.experimental.pallas import tpu as pltpu
from jax.sharding import PartitionSpec as P

LEN = 512
MESH = pl.DeviceIdType.MESH
AHEAD = 2


def gradient_kernel(n, groups, examples, width, *refs):
    values, factors, out = refs[:5], refs[5:10], refs[10]
    held, weights = refs[11:16], refs[16:21]
    (terms, arrived, pieces, rows_in, shared, load_sem, weight_sem,
     send_sem, recv_sem, send2, recv2, send3, recv3) = refs[21:]
    me, lane = lax.axis_index("tensor"), lax.axis_index("dp")
    tokens = terms.shape[1]
    rows = width // n

    def load(step, k):
        owner = lax.rem(me + 1 + step, n)
        start = pl.multiple_of(owner * tokens, tokens)
        return pltpu.make_async_copy(
            values[k].at[pl.ds(start, tokens)], held[k].at[step], load_sem.at[step, k]
        )

    def weight(k):
        return pltpu.make_async_copy(factors[k], weights[k], weight_sem.at[k])

    for k in range(5):
        weight(k).start()
        load(0, k).start()
    for step in range(1, min(AHEAD, n)):
        for k in range(5):
            load(step, k).start()

    barrier = pltpu.get_barrier_semaphore()
    for hop in range(1, n):
        pl.semaphore_signal(barrier, inc=1, device_id={"tensor": lax.rem(me + hop, n)}, device_id_type=MESH)
    for hop in range(1, groups):
        pl.semaphore_signal(barrier, inc=1, device_id={"dp": lax.rem(lane + hop, groups)}, device_id_type=MESH)
    pl.semaphore_wait(barrier, n + groups - 2)
    for k in range(5):
        weight(k).wait()

    def send(step):
        return pltpu.make_async_remote_copy(
            src_ref=terms.at[step],
            dst_ref=arrived.at[step],
            send_sem=send_sem.at[step],
            recv_sem=recv_sem.at[step],
            device_id={"tensor": lax.rem(me + 1 + step, n)},
            device_id_type=MESH,
        )

    def project(step, carry):
        @pl.when(step + AHEAD < n)
        def _():
            for k in range(5):
                load(step + AHEAD, k).start()

        column = 0
        for k in range(5):
            load(step, k).wait()
            share = weights[k].shape[1]
            terms[step, :, column : column + share] = jnp.dot(
                held[k][step], weights[k][...], preferred_element_type=jnp.float32
            )
            column += share

        @pl.when(step < n - 1)
        def _():
            send(step).start()

        return carry

    lax.fori_loop(0, n, project, 0)

    total = terms[n - 1]
    for step in range(n - 1):
        send(step).wait_recv()
        total = total + arrived[step]
    product = lax.dot_general(
        total[:, 3 * width :],
        total[:, : 3 * width],
        (((0,), (0,)), ((), ())),
        precision=lax.Precision.HIGHEST,
        preferred_element_type=jnp.float32,
    ) * (LEN ** -0.5)
    for peer in range(n):
        for m in range(3):
            first = m * width + peer * rows
            pieces[peer, m] = product[first : first + rows, m * width : (m + 1) * width]

    def send_rows(hop):
        peer = lax.rem(me + hop, n)
        return pltpu.make_async_remote_copy(
            src_ref=pieces.at[peer],
            dst_ref=rows_in.at[me],
            send_sem=send2.at[hop - 1],
            recv_sem=recv2.at[hop - 1],
            device_id={"tensor": peer},
            device_id_type=MESH,
        )

    for hop in range(1, n):
        send_rows(hop).start()
    rows_in[me] = pieces[me]
    for hop in range(1, n):
        send_rows(hop).wait_recv()
    each = n // examples
    for e in range(examples):
        done = rows_in[e * each]
        for source in range(e * each + 1, (e + 1) * each):
            done = done + rows_in[source]
        shared[lane, e] = done

    def share(hop):
        return pltpu.make_async_remote_copy(
            src_ref=shared.at[lane],
            dst_ref=shared.at[lane],
            send_sem=send3.at[hop - 1],
            recv_sem=recv3.at[hop - 1],
            device_id={"dp": lax.rem(lane + hop, groups)},
            device_id_type=MESH,
        )

    for hop in range(1, groups):
        share(hop).start()
    for hop in range(1, groups):
        share(hop).wait_recv()
    out[...] = shared[...]
    for step in range(n - 1):
        send(step).wait_send()
    for hop in range(1, n):
        send_rows(hop).wait_send()
    for hop in range(1, groups):
        share(hop).wait_send()


def score_kernel(n, groups, examples, terms, out, blocks, arrived, send_sem, recv_sem):
    me, lane = lax.axis_index("tensor"), lax.axis_index("dp")
    split = n // groups
    columns = out.shape[1]
    source = me // split
    own = lane == source

    barrier = pltpu.get_barrier_semaphore()
    for t in range(n):
        @pl.when(jnp.logical_not(own & (me == t)))
        def _(t=t):
            pl.semaphore_signal(barrier, inc=1, device_id={"dp": source, "tensor": t}, device_id_type=MESH)

    for b in range(groups):
        for s in range(split):
            blocks[b * split + s] = (
                terms[b * examples : (b + 1) * examples, s * columns : (s + 1) * columns]
                + terms[
                    (groups + b) * examples : (groups + b + 1) * examples,
                    s * columns : (s + 1) * columns,
                ]
            )

    @pl.when(own)
    def _():
        pl.semaphore_wait(barrier, n - 1)

    @pl.when(jnp.logical_not(own))
    def _():
        pl.semaphore_wait(barrier, n)

    def send(b, s):
        return pltpu.make_async_remote_copy(
            src_ref=blocks.at[b * split + s],
            dst_ref=arrived.at[me],
            send_sem=send_sem.at[b * split + s],
            recv_sem=recv_sem.at[me],
            device_id={"dp": b, "tensor": lane * split + s},
            device_id_type=MESH,
        )

    def to_me(b, s):
        return (lane == b) & (me == lane * split + s)

    for b in range(groups):
        for s in range(split):
            @pl.when(jnp.logical_not(to_me(b, s)))
            def _(b=b, s=s):
                send(b, s).start()

            @pl.when(to_me(b, s))
            def _(b=b, s=s):
                arrived[me] = blocks[b * split + s]

    def wait_from(t):
        pltpu.make_async_remote_copy(
            src_ref=blocks.at[0],
            dst_ref=arrived.at[t],
            send_sem=send_sem.at[0],
            recv_sem=recv_sem.at[t],
            device_id={"dp": source, "tensor": t},
            device_id_type=MESH,
        ).wait_recv()

    for t in range(n):
        @pl.when(jnp.logical_not(own & (me == t)))
        def _(t=t):
            wait_from(t)

    total = arrived[0]
    for t in range(1, n):
        total = total + arrived[t]
    out[...] = total
    for b in range(groups):
        for s in range(split):
            @pl.when(jnp.logical_not(to_me(b, s)))
            def _(b=b, s=s):
                send(b, s).wait_send()


def shards(n, groups, *arrays):
    values, factors, queries = arrays[:5], arrays[5:10], arrays[10]
    width = factors[1].shape[1]
    local = values[0].shape[0]
    examples, tokens, rows = local // LEN, local // n, width // n
    f32, bf16 = jnp.float32, jnp.bfloat16
    dma = pltpu.SemaphoreType.DMA
    gradients = pl.pallas_call(
        functools.partial(gradient_kernel, n, groups, examples, width),
        out_shape=jax.ShapeDtypeStruct((groups, examples, 3, rows, width), f32),
        in_specs=[pl.BlockSpec(memory_space=pl.ANY)] * 10,
        out_specs=pl.BlockSpec(memory_space=pltpu.VMEM),
        scratch_shapes=[pltpu.VMEM((n, tokens, v.shape[1]), bf16) for v in values]
        + [pltpu.VMEM(w.shape, bf16) for w in factors]
        + [
            pltpu.VMEM((n, tokens, 6 * width), f32),
            pltpu.VMEM((n - 1, tokens, 6 * width), f32),
            pltpu.VMEM((n, 3, rows, width), f32),
            pltpu.VMEM((n, 3, rows, width), f32),
            pltpu.VMEM((groups, examples, 3, rows, width), f32),
            dma((n, 5)),
            dma((5,)),
            dma((n - 1,)),
            dma((n - 1,)),
            dma((n - 1,)),
            dma((n - 1,)),
            dma((groups - 1,)),
            dma((groups - 1,)),
        ],
        compiler_params=pltpu.CompilerParams(
            collective_id=0, has_side_effects=True, vmem_limit_bytes=56 * 2**20
        ),
    )(values[0], values[1], values[2], values[3], values[4], *factors)
    gradients = gradients.reshape(groups * examples, 3, rows * width)
    high = lax.reduce_precision(gradients, 8, 7)
    low = gradients - high
    both = jnp.concatenate([high, low], 0).astype(bf16)
    terms = jnp.einsum("emv,qmv->eq", both, queries, preferred_element_type=f32)
    columns = terms.shape[1] * groups // n
    return pl.pallas_call(
        functools.partial(score_kernel, n, groups, examples),
        out_shape=jax.ShapeDtypeStruct((examples, columns), f32),
        in_specs=[pl.BlockSpec(memory_space=pltpu.VMEM)],
        out_specs=pl.BlockSpec(memory_space=pltpu.VMEM),
        scratch_shapes=[
            pltpu.VMEM((n, examples, columns), f32),
            pltpu.VMEM((n, examples, columns), f32),
            dma((n,)),
            dma((n,)),
        ],
        compiler_params=pltpu.CompilerParams(collective_id=1, has_side_effects=True),
    )(terms)


def solution(mesh):
    placed = (
        P(("parts", "dp"), "tensor"),
        P(("parts", "dp"), "tensor"),
        P(("parts", "dp"), "tensor"),
        P(("parts", "dp"), "tensor"),
        P(("parts", "dp"), "tensor"),
        P("tensor", None),
        P("tensor", None),
        P("tensor", None),
        P("tensor", None),
        P("tensor", None),
        P("dp", None, "tensor"),
    )
    return jax.shard_map(
        functools.partial(shards, mesh.shape["tensor"], mesh.shape["dp"]),
        mesh=mesh,
        in_specs=placed,
        out_specs=P(("parts", "dp"), "tensor"),
        check_vma=False,
    )
```

```python
import functools

import jax
import jax.numpy as jnp
from jax import lax
from jax.experimental import pallas as pl
from jax.experimental.pallas import tpu as pltpu
from jax.sharding import PartitionSpec as P

LEN = 512
MESH = pl.DeviceIdType.MESH
AHEAD = 2
CHUNKS = 4
CHUNK = LEN // CHUNKS


def gradient_kernel(n, groups, width, *refs):
    values, factors, out = refs[:5], refs[5:10], refs[10]
    held, weights = refs[11:16], refs[16:21]
    (terms, arrived, pieces, shared, load_sem, weight_sem,
     send_sem, recv_sem, spread_send, spread_recv) = refs[21:]
    me, lane = lax.axis_index("tensor"), lax.axis_index("dp")
    rows = width // n
    last = n - 1
    at_end = (me == 0) | (me == last)
    mine = jnp.where(me == 0, 0, 1)

    def load(step, k, example):
        start = pl.multiple_of(example * LEN + step * CHUNK, CHUNK)
        return pltpu.make_async_copy(
            values[k].at[pl.ds(start, CHUNK)],
            held[k].at[step, pl.ds(example * CHUNK, CHUNK)],
            load_sem.at[step, k, example],
        )

    def weight(k):
        return pltpu.make_async_copy(factors[k], weights[k], weight_sem.at[k])

    for step in range(AHEAD):
        for k in range(5):
            if step == 0:
                weight(k).start()
            load(step, k, 0).start()
            load(step, k, 1).start()

    barrier = pltpu.get_barrier_semaphore()

    def greet(there, target):
        @pl.when(there)
        def _():
            pl.semaphore_signal(barrier, inc=1, device_id=target, device_id_type=MESH)

    greet(me > 0, {"dp": lane, "tensor": jnp.maximum(me - 1, 0)})
    greet(me < last, {"dp": lane, "tensor": jnp.minimum(me + 1, last)})
    for b in range(groups):
        for end in (0, last):
            greet(jnp.logical_not((lane == b) & (me == end)), {"dp": b, "tensor": end})

    @pl.when(at_end)
    def _():
        pl.semaphore_wait(barrier, n * groups)

    @pl.when(jnp.logical_not(at_end))
    def _():
        pl.semaphore_wait(barrier, 2)

    for k in range(5):
        weight(k).wait()

    def send(example, chunk):
        target = jnp.maximum(me - 1, 0) if example == 0 else jnp.minimum(me + 1, last)
        return pltpu.make_async_remote_copy(
            src_ref=terms.at[chunk, pl.ds(example * CHUNK, CHUNK)],
            dst_ref=arrived.at[chunk, pl.ds(example * CHUNK, CHUNK)],
            send_sem=send_sem.at[example, chunk],
            recv_sem=recv_sem.at[example, chunk],
            device_id={"dp": lane, "tensor": target},
            device_id_type=MESH,
        )

    def advance(step, carry):
        @pl.when(step + AHEAD < CHUNKS)
        def _():
            for k in range(5):
                load(step + AHEAD, k, 0).start()
                load(step + AHEAD, k, 1).start()

        @pl.when(step < CHUNKS)
        def _():
            column = 0
            for k in range(5):
                load(step, k, 0).wait()
                load(step, k, 1).wait()
                turned = 1 if k else 0
                share = weights[k].shape[1 - turned]
                terms[step, :, column : column + share] = lax.dot_general(
                    held[k][step],
                    weights[k][...],
                    (((1,), (turned,)), ((), ())),
                    preferred_element_type=jnp.float32,
                )
                column += share

        for example in range(2):
            hops = last - me if example == 0 else me
            chunk = step - hops
            part = slice(example * CHUNK, (example + 1) * CHUNK)

            @pl.when((chunk >= 0) & (chunk < CHUNKS))
            def _(example=example, hops=hops, chunk=chunk, part=part):
                @pl.when(hops > 0)
                def _():
                    send(example, chunk).wait_recv()
                    terms[chunk, part, :] = terms[chunk, part, :] + arrived[chunk, part, :]

                @pl.when(hops < last)
                def _():
                    send(example, chunk).start()

        return carry

    lax.fori_loop(0, CHUNKS + last, advance, 0)

    def spread(b, peer):
        return pltpu.make_async_remote_copy(
            src_ref=pieces.at[peer],
            dst_ref=shared.at[lane, mine],
            send_sem=spread_send.at[b, peer],
            recv_sem=spread_recv.at[lane, mine],
            device_id={"dp": b, "tensor": peer},
            device_id_type=MESH,
        )

    def to_others(action):
        def visit(q, carry):
            b, peer = q // n, lax.rem(q, n)

            @pl.when(jnp.logical_not((b == lane) & (peer == me)))
            def _():
                action(spread(b, peer))

            return carry

        lax.fori_loop(0, groups * n, visit, 0)

    @pl.when(at_end)
    def _():
        start = pl.multiple_of(mine * CHUNK, CHUNK)
        total = terms[:, pl.ds(start, CHUNK), :].reshape(LEN, 6 * width)
        product = lax.dot_general(
            total[:, 3 * width :],
            total[:, : 3 * width],
            (((0,), (0,)), ((), ())),
            precision=lax.Precision.HIGHEST,
            preferred_element_type=jnp.float32,
        ) * (LEN ** -0.5)
        for peer in range(n):
            for m in range(3):
                first = m * width + peer * rows
                pieces[peer, m] = product[first : first + rows, m * width : (m + 1) * width]
        to_others(lambda copy: copy.start())
        shared[lane, mine] = pieces[me]

    for b in range(groups):
        for example, end in enumerate((0, last)):
            @pl.when(jnp.logical_not((lane == b) & (me == end)))
            def _(b=b, example=example, end=end):
                pltpu.make_async_remote_copy(
                    src_ref=pieces.at[0],
                    dst_ref=shared.at[b, example],
                    send_sem=spread_send.at[0, 0],
                    recv_sem=spread_recv.at[b, example],
                    device_id={"dp": b, "tensor": end},
                    device_id_type=MESH,
                ).wait_recv()

    out[...] = shared[...]

    @pl.when(at_end)
    def _():
        to_others(lambda copy: copy.wait_send())

    for chunk in range(CHUNKS):
        @pl.when(me > 0)
        def _(chunk=chunk):
            send(0, chunk).wait_send()

        @pl.when(me < last)
        def _(chunk=chunk):
            send(1, chunk).wait_send()


def score_kernel(n, groups, examples, terms, out, blocks, arrived, send_sem, recv_sem):
    me, lane = lax.axis_index("tensor"), lax.axis_index("dp")
    split = n // groups
    columns = out.shape[1]
    source = me // split
    own = lane == source

    barrier = pltpu.get_barrier_semaphore()
    for t in range(n):
        @pl.when(jnp.logical_not(own & (me == t)))
        def _(t=t):
            pl.semaphore_signal(barrier, inc=1, device_id={"dp": source, "tensor": t}, device_id_type=MESH)

    for b in range(groups):
        for s in range(split):
            blocks[b * split + s] = (
                terms[b * examples : (b + 1) * examples, s * columns : (s + 1) * columns]
                + terms[
                    (groups + b) * examples : (groups + b + 1) * examples,
                    s * columns : (s + 1) * columns,
                ]
            )

    @pl.when(own)
    def _():
        pl.semaphore_wait(barrier, n - 1)

    @pl.when(jnp.logical_not(own))
    def _():
        pl.semaphore_wait(barrier, n)

    def send(b, s):
        return pltpu.make_async_remote_copy(
            src_ref=blocks.at[b * split + s],
            dst_ref=arrived.at[me],
            send_sem=send_sem.at[b * split + s],
            recv_sem=recv_sem.at[me],
            device_id={"dp": b, "tensor": lane * split + s},
            device_id_type=MESH,
        )

    def to_me(b, s):
        return (lane == b) & (me == lane * split + s)

    for b in range(groups):
        for s in range(split):
            @pl.when(jnp.logical_not(to_me(b, s)))
            def _(b=b, s=s):
                send(b, s).start()

            @pl.when(to_me(b, s))
            def _(b=b, s=s):
                arrived[me] = blocks[b * split + s]

    def wait_from(t):
        pltpu.make_async_remote_copy(
            src_ref=blocks.at[0],
            dst_ref=arrived.at[t],
            send_sem=send_sem.at[0],
            recv_sem=recv_sem.at[t],
            device_id={"dp": source, "tensor": t},
            device_id_type=MESH,
        ).wait_recv()

    for t in range(n):
        @pl.when(jnp.logical_not(own & (me == t)))
        def _(t=t):
            wait_from(t)

    total = arrived[0]
    for t in range(1, n):
        total = total + arrived[t]
    out[...] = total
    for b in range(groups):
        for s in range(split):
            @pl.when(jnp.logical_not(to_me(b, s)))
            def _(b=b, s=s):
                send(b, s).wait_send()


def shards(n, groups, *arrays):
    values, factors, queries = arrays[:5], arrays[5:10], arrays[10]
    width = factors[1].shape[1]
    local = values[0].shape[0]
    examples, rows = local // LEN, width // n
    f32, bf16 = jnp.float32, jnp.bfloat16
    dma = pltpu.SemaphoreType.DMA
    turned = [factors[0]] + [w.T for w in factors[1:]]
    gradients = pl.pallas_call(
        functools.partial(gradient_kernel, n, groups, width),
        out_shape=jax.ShapeDtypeStruct((groups, examples, 3, rows, width), f32),
        in_specs=[pl.BlockSpec(memory_space=pl.ANY)] * 10,
        out_specs=pl.BlockSpec(memory_space=pltpu.VMEM),
        scratch_shapes=[pltpu.VMEM((CHUNKS, 2 * CHUNK, v.shape[1]), bf16) for v in values]
        + [pltpu.VMEM(w.shape, bf16) for w in turned]
        + [
            pltpu.VMEM((CHUNKS, 2 * CHUNK, 6 * width), f32),
            pltpu.VMEM((CHUNKS, 2 * CHUNK, 6 * width), f32),
            pltpu.VMEM((n, 3, rows, width), f32),
            pltpu.VMEM((groups, examples, 3, rows, width), f32),
            dma((CHUNKS, 5, 2)),
            dma((5,)),
            dma((2, CHUNKS)),
            dma((2, CHUNKS)),
            dma((groups, n)),
            dma((groups, examples)),
        ],
        compiler_params=pltpu.CompilerParams(
            collective_id=0, has_side_effects=True, vmem_limit_bytes=56 * 2**20
        ),
    )(*values, *turned)
    gradients = gradients.reshape(groups * examples, 3, rows * width)
    high = lax.reduce_precision(gradients, 8, 7)
    low = gradients - high
    both = jnp.concatenate([high, low], 0).astype(bf16)
    terms = jnp.einsum("emv,qmv->eq", both, queries, preferred_element_type=f32)
    columns = terms.shape[1] * groups // n
    return pl.pallas_call(
        functools.partial(score_kernel, n, groups, examples),
        out_shape=jax.ShapeDtypeStruct((examples, columns), f32),
        in_specs=[pl.BlockSpec(memory_space=pltpu.VMEM)],
        out_specs=pl.BlockSpec(memory_space=pltpu.VMEM),
        scratch_shapes=[
            pltpu.VMEM((n, examples, columns), f32),
            pltpu.VMEM((n, examples, columns), f32),
            dma((n,)),
            dma((n,)),
        ],
        compiler_params=pltpu.CompilerParams(collective_id=1, has_side_effects=True),
    )(terms)


def solution(mesh):
    placed = (
        P(("parts", "dp"), "tensor"),
        P(("parts", "dp"), "tensor"),
        P(("parts", "dp"), "tensor"),
        P(("parts", "dp"), "tensor"),
        P(("parts", "dp"), "tensor"),
        P("tensor", None),
        P("tensor", None),
        P("tensor", None),
        P("tensor", None),
        P("tensor", None),
        P("dp", None, "tensor"),
    )
    return jax.shard_map(
        functools.partial(shards, mesh.shape["tensor"], mesh.shape["dp"]),
        mesh=mesh,
        in_specs=placed,
        out_specs=P(("parts", "dp"), "tensor"),
        check_vma=False,
    )
```

```python
import functools

import jax
import jax.numpy as jnp
from jax import lax
from jax.experimental import pallas as pl
from jax.experimental.pallas import tpu as pltpu
from jax.sharding import PartitionSpec as P

LEN = 512
MESH = pl.DeviceIdType.MESH
AHEAD = 2
CHUNKS = 4
CHUNK = LEN // CHUNKS
PIECES = 4
PIECE = CHUNK // PIECES


def gradient_kernel(n, groups, width, *refs):
    values, factors, out = refs[:5], refs[5:10], refs[10]
    held, weights = refs[11:16], refs[16:21]
    (terms, arrived, pieces, shared, load_sem, weight_sem,
     send_sem, recv_sem, spread_send, spread_recv) = refs[21:]
    me, lane = lax.axis_index("tensor"), lax.axis_index("dp")
    rows = width // n
    last = n - 1
    at_end = (me == 0) | (me == last)
    mine = jnp.where(me == 0, 0, 1)

    def load(step, k, example):
        start = pl.multiple_of(example * LEN + step * CHUNK, CHUNK)
        return pltpu.make_async_copy(
            values[k].at[pl.ds(start, CHUNK)],
            held[k].at[step, pl.ds(example * CHUNK, CHUNK)],
            load_sem.at[step, k, example],
        )

    def weight(k):
        return pltpu.make_async_copy(factors[k], weights[k], weight_sem.at[k])

    for step in range(AHEAD):
        for k in range(5):
            if step == 0:
                weight(k).start()
            load(step, k, 0).start()
            load(step, k, 1).start()

    barrier = pltpu.get_barrier_semaphore()

    def greet(there, target):
        @pl.when(there)
        def _():
            pl.semaphore_signal(barrier, inc=1, device_id=target, device_id_type=MESH)

    greet(me > 0, {"dp": lane, "tensor": jnp.maximum(me - 1, 0)})
    greet(me < last, {"dp": lane, "tensor": jnp.minimum(me + 1, last)})
    for b in range(groups):
        for end in (0, last):
            greet(jnp.logical_not((lane == b) & (me == end)), {"dp": b, "tensor": end})

    @pl.when(at_end)
    def _():
        pl.semaphore_wait(barrier, n * groups)

    @pl.when(jnp.logical_not(at_end))
    def _():
        pl.semaphore_wait(barrier, 2)

    for k in range(5):
        weight(k).wait()

    def send(example, chunk, piece):
        target = jnp.maximum(me - 1, 0) if example == 0 else jnp.minimum(me + 1, last)
        part = pl.ds(example * CHUNK + piece * PIECE, PIECE)
        return pltpu.make_async_remote_copy(
            src_ref=terms.at[chunk, part],
            dst_ref=arrived.at[chunk, part],
            send_sem=send_sem.at[example, chunk, piece],
            recv_sem=recv_sem.at[example, chunk, piece],
            device_id={"dp": lane, "tensor": target},
            device_id_type=MESH,
        )

    def advance(step, carry):
        @pl.when(step + AHEAD < CHUNKS)
        def _():
            for k in range(5):
                load(step + AHEAD, k, 0).start()
                load(step + AHEAD, k, 1).start()

        @pl.when(step < CHUNKS)
        def _():
            column = 0
            for k in range(5):
                load(step, k, 0).wait()
                load(step, k, 1).wait()
                turned = 1 if k else 0
                share = weights[k].shape[1 - turned]
                terms[step, :, column : column + share] = lax.dot_general(
                    held[k][step],
                    weights[k][...],
                    (((1,), (turned,)), ((), ())),
                    preferred_element_type=jnp.float32,
                )
                column += share

        for piece in range(PIECES):
            for example in range(2):
                hops = last - me if example == 0 else me
                chunk = step - hops
                first = example * CHUNK + piece * PIECE
                part = slice(first, first + PIECE)
                active = (chunk >= 0) & (chunk < CHUNKS)

                @pl.when(active & (hops > 0))
                def _(example=example, chunk=chunk, piece=piece, part=part):
                    send(example, chunk, piece).wait_recv()
                    terms[chunk, part, :] = terms[chunk, part, :] + arrived[chunk, part, :]

                @pl.when(active & (hops < last))
                def _(example=example, chunk=chunk, piece=piece):
                    send(example, chunk, piece).start()

        return carry

    lax.fori_loop(0, CHUNKS + last, advance, 0)

    def spread(b, peer):
        return pltpu.make_async_remote_copy(
            src_ref=pieces.at[peer],
            dst_ref=shared.at[lane, mine],
            send_sem=spread_send.at[b, peer],
            recv_sem=spread_recv.at[lane, mine],
            device_id={"dp": b, "tensor": peer},
            device_id_type=MESH,
        )

    def to_others(action):
        def visit(q, carry):
            b, peer = q // n, lax.rem(q, n)

            @pl.when(jnp.logical_not((b == lane) & (peer == me)))
            def _():
                action(spread(b, peer))

            return carry

        lax.fori_loop(0, groups * n, visit, 0)

    @pl.when(at_end)
    def _():
        start = pl.multiple_of(mine * CHUNK, CHUNK)
        total = terms[:, pl.ds(start, CHUNK), :].reshape(LEN, 6 * width)
        product = lax.dot_general(
            total[:, 3 * width :],
            total[:, : 3 * width],
            (((0,), (0,)), ((), ())),
            precision=lax.Precision.HIGHEST,
            preferred_element_type=jnp.float32,
        ) * (LEN ** -0.5)
        for peer in range(n):
            for m in range(3):
                first = m * width + peer * rows
                pieces[peer, m] = product[first : first + rows, m * width : (m + 1) * width]
        to_others(lambda copy: copy.start())
        shared[lane, mine] = pieces[me]

    for b in range(groups):
        for example, end in enumerate((0, last)):
            @pl.when(jnp.logical_not((lane == b) & (me == end)))
            def _(b=b, example=example, end=end):
                pltpu.make_async_remote_copy(
                    src_ref=pieces.at[0],
                    dst_ref=shared.at[b, example],
                    send_sem=spread_send.at[0, 0],
                    recv_sem=spread_recv.at[b, example],
                    device_id={"dp": b, "tensor": end},
                    device_id_type=MESH,
                ).wait_recv()

    out[...] = shared[...]

    @pl.when(at_end)
    def _():
        to_others(lambda copy: copy.wait_send())

    for chunk in range(CHUNKS):
        for piece in range(PIECES):
            @pl.when(me > 0)
            def _(chunk=chunk, piece=piece):
                send(0, chunk, piece).wait_send()

            @pl.when(me < last)
            def _(chunk=chunk, piece=piece):
                send(1, chunk, piece).wait_send()


def score_kernel(n, groups, examples, terms, out, blocks, arrived, send_sem, recv_sem):
    me, lane = lax.axis_index("tensor"), lax.axis_index("dp")
    split = n // groups
    columns = out.shape[1]
    source = me // split
    own = lane == source

    barrier = pltpu.get_barrier_semaphore()
    for t in range(n):
        @pl.when(jnp.logical_not(own & (me == t)))
        def _(t=t):
            pl.semaphore_signal(barrier, inc=1, device_id={"dp": source, "tensor": t}, device_id_type=MESH)

    for b in range(groups):
        for s in range(split):
            blocks[b * split + s] = (
                terms[b * examples : (b + 1) * examples, s * columns : (s + 1) * columns]
                + terms[
                    (groups + b) * examples : (groups + b + 1) * examples,
                    s * columns : (s + 1) * columns,
                ]
            )

    @pl.when(own)
    def _():
        pl.semaphore_wait(barrier, n - 1)

    @pl.when(jnp.logical_not(own))
    def _():
        pl.semaphore_wait(barrier, n)

    def send(b, s):
        return pltpu.make_async_remote_copy(
            src_ref=blocks.at[b * split + s],
            dst_ref=arrived.at[me],
            send_sem=send_sem.at[b * split + s],
            recv_sem=recv_sem.at[me],
            device_id={"dp": b, "tensor": lane * split + s},
            device_id_type=MESH,
        )

    def to_me(b, s):
        return (lane == b) & (me == lane * split + s)

    for b in range(groups):
        for s in range(split):
            @pl.when(jnp.logical_not(to_me(b, s)))
            def _(b=b, s=s):
                send(b, s).start()

            @pl.when(to_me(b, s))
            def _(b=b, s=s):
                arrived[me] = blocks[b * split + s]

    def wait_from(t):
        pltpu.make_async_remote_copy(
            src_ref=blocks.at[0],
            dst_ref=arrived.at[t],
            send_sem=send_sem.at[0],
            recv_sem=recv_sem.at[t],
            device_id={"dp": source, "tensor": t},
            device_id_type=MESH,
        ).wait_recv()

    for t in range(n):
        @pl.when(jnp.logical_not(own & (me == t)))
        def _(t=t):
            wait_from(t)

    total = arrived[0]
    for t in range(1, n):
        total = total + arrived[t]
    out[...] = total
    for b in range(groups):
        for s in range(split):
            @pl.when(jnp.logical_not(to_me(b, s)))
            def _(b=b, s=s):
                send(b, s).wait_send()


def shards(n, groups, *arrays):
    values, factors, queries = arrays[:5], arrays[5:10], arrays[10]
    width = factors[1].shape[1]
    local = values[0].shape[0]
    examples, rows = local // LEN, width // n
    f32, bf16 = jnp.float32, jnp.bfloat16
    dma = pltpu.SemaphoreType.DMA
    turned = [factors[0]] + [w.T for w in factors[1:]]
    gradients = pl.pallas_call(
        functools.partial(gradient_kernel, n, groups, width),
        out_shape=jax.ShapeDtypeStruct((groups, examples, 3, rows, width), f32),
        in_specs=[pl.BlockSpec(memory_space=pl.ANY)] * 10,
        out_specs=pl.BlockSpec(memory_space=pltpu.VMEM),
        scratch_shapes=[pltpu.VMEM((CHUNKS, 2 * CHUNK, v.shape[1]), bf16) for v in values]
        + [pltpu.VMEM(w.shape, bf16) for w in turned]
        + [
            pltpu.VMEM((CHUNKS, 2 * CHUNK, 6 * width), f32),
            pltpu.VMEM((CHUNKS, 2 * CHUNK, 6 * width), f32),
            pltpu.VMEM((n, 3, rows, width), f32),
            pltpu.VMEM((groups, examples, 3, rows, width), f32),
            dma((CHUNKS, 5, 2)),
            dma((5,)),
            dma((2, CHUNKS, PIECES)),
            dma((2, CHUNKS, PIECES)),
            dma((groups, n)),
            dma((groups, examples)),
        ],
        compiler_params=pltpu.CompilerParams(
            collective_id=0, has_side_effects=True, vmem_limit_bytes=56 * 2**20
        ),
    )(*values, *turned)
    gradients = gradients.reshape(groups * examples, 3, rows * width)
    high = lax.reduce_precision(gradients, 8, 7)
    low = gradients - high
    both = jnp.concatenate([high, low], 0).astype(bf16)
    terms = jnp.einsum("emv,qmv->eq", both, queries, preferred_element_type=f32)
    columns = terms.shape[1] * groups // n
    return pl.pallas_call(
        functools.partial(score_kernel, n, groups, examples),
        out_shape=jax.ShapeDtypeStruct((examples, columns), f32),
        in_specs=[pl.BlockSpec(memory_space=pltpu.VMEM)],
        out_specs=pl.BlockSpec(memory_space=pltpu.VMEM),
        scratch_shapes=[
            pltpu.VMEM((n, examples, columns), f32),
            pltpu.VMEM((n, examples, columns), f32),
            dma((n,)),
            dma((n,)),
        ],
        compiler_params=pltpu.CompilerParams(collective_id=1, has_side_effects=True),
    )(terms)


def solution(mesh):
    placed = (
        P(("parts", "dp"), "tensor"),
        P(("parts", "dp"), "tensor"),
        P(("parts", "dp"), "tensor"),
        P(("parts", "dp"), "tensor"),
        P(("parts", "dp"), "tensor"),
        P("tensor", None),
        P("tensor", None),
        P("tensor", None),
        P("tensor", None),
        P("tensor", None),
        P("dp", None, "tensor"),
    )
    return jax.shard_map(
        functools.partial(shards, mesh.shape["tensor"], mesh.shape["dp"]),
        mesh=mesh,
        in_specs=placed,
        out_specs=P(("parts", "dp"), "tensor"),
        check_vma=False,
    )
```

```python
import functools

import jax
import jax.numpy as jnp
from jax import lax
from jax.experimental import pallas as pl
from jax.experimental.pallas import tpu as pltpu
from jax.sharding import PartitionSpec as P

LEN = 512
MESH = pl.DeviceIdType.MESH
AHEAD = 1
CHUNKS = 4
CHUNK = LEN // CHUNKS
PIECES = 4
PIECE = CHUNK // PIECES


def gradient_kernel(n, groups, width, *refs):
    values, factors, out = refs[:5], refs[5:10], refs[10]
    held, weights = refs[11:16], refs[16:21]
    (terms, arrived, pieces, shared, load_sem, weight_sem,
     send_sem, recv_sem, spread_send, spread_recv) = refs[21:31]
    upright = refs[31:]
    me, lane = lax.axis_index("tensor"), lax.axis_index("dp")
    rows = width // n
    last = n - 1
    at_end = (me == 0) | (me == last)
    mine = jnp.where(me == 0, 0, 1)

    def load(step, k, example):
        start = pl.multiple_of(example * LEN + step * CHUNK, CHUNK)
        return pltpu.make_async_copy(
            values[k].at[pl.ds(start, CHUNK)],
            held[k].at[step, pl.ds(example * CHUNK, CHUNK)],
            load_sem.at[step, k, example],
        )

    def weight(k):
        return pltpu.make_async_copy(factors[k], weights[k], weight_sem.at[k])

    for step in range(AHEAD):
        for k in range(5):
            if step == 0:
                weight(k).start()
            load(step, k, 0).start()
            load(step, k, 1).start()

    barrier = pltpu.get_barrier_semaphore()

    def greet(there, target):
        @pl.when(there)
        def _():
            pl.semaphore_signal(barrier, inc=1, device_id=target, device_id_type=MESH)

    greet(me > 0, {"dp": lane, "tensor": jnp.maximum(me - 1, 0)})
    greet(me < last, {"dp": lane, "tensor": jnp.minimum(me + 1, last)})
    for b in range(groups):
        for end in (0, last):
            greet(jnp.logical_not((lane == b) & (me == end)), {"dp": b, "tensor": end})

    @pl.when(at_end)
    def _():
        pl.semaphore_wait(barrier, n * groups)

    @pl.when(jnp.logical_not(at_end))
    def _():
        pl.semaphore_wait(barrier, 2)

    for k in range(5):
        weight(k).wait()
        if k:
            upright[k - 1][...] = weights[k][...].T

    def send(example, chunk, piece):
        target = jnp.maximum(me - 1, 0) if example == 0 else jnp.minimum(me + 1, last)
        part = pl.ds(example * CHUNK + piece * PIECE, PIECE)
        return pltpu.make_async_remote_copy(
            src_ref=terms.at[chunk, part],
            dst_ref=arrived.at[chunk, part],
            send_sem=send_sem.at[example, chunk, piece],
            recv_sem=recv_sem.at[example, chunk, piece],
            device_id={"dp": lane, "tensor": target},
            device_id_type=MESH,
        )

    def advance(step, carry):
        @pl.when(step < CHUNKS)
        def _():
            column = 0
            for k in range(5):
                load(step, k, 0).wait()
                load(step, k, 1).wait()

                @pl.when(step + AHEAD < CHUNKS)
                def _(k=k):
                    load(step + AHEAD, k, 0).start()
                    load(step + AHEAD, k, 1).start()

                turned = 1 if k else 0
                share = weights[k].shape[1 - turned]
                terms[step, :, column : column + share] = lax.dot_general(
                    held[k][step],
                    upright[k - 1][...] if k else weights[k][...],
                    (((1,), (0,)), ((), ())),
                    preferred_element_type=jnp.float32,
                )
                column += share

        for piece in range(PIECES):
            for example in range(2):
                hops = last - me if example == 0 else me
                chunk = step - hops
                first = example * CHUNK + piece * PIECE
                part = slice(first, first + PIECE)
                active = (chunk >= 0) & (chunk < CHUNKS)

                @pl.when(active & (hops > 0))
                def _(example=example, chunk=chunk, piece=piece, part=part):
                    send(example, chunk, piece).wait_recv()
                    terms[chunk, part, :] = terms[chunk, part, :] + arrived[chunk, part, :]

                @pl.when(active & (hops < last))
                def _(example=example, chunk=chunk, piece=piece):
                    send(example, chunk, piece).start()

        return carry

    lax.fori_loop(0, CHUNKS + last, advance, 0)

    def spread(b, peer):
        return pltpu.make_async_remote_copy(
            src_ref=pieces.at[peer],
            dst_ref=shared.at[lane, mine],
            send_sem=spread_send.at[b, peer],
            recv_sem=spread_recv.at[lane, mine],
            device_id={"dp": b, "tensor": peer},
            device_id_type=MESH,
        )

    def to_others(action):
        def visit(q, carry):
            b, peer = q // n, lax.rem(q, n)

            @pl.when(jnp.logical_not((b == lane) & (peer == me)))
            def _():
                action(spread(b, peer))

            return carry

        lax.fori_loop(0, groups * n, visit, 0)

    @pl.when(at_end)
    def _():
        start = pl.multiple_of(mine * CHUNK, CHUNK)
        total = terms[:, pl.ds(start, CHUNK), :].reshape(LEN, 6 * width)
        product = lax.dot_general(
            total[:, 3 * width :],
            total[:, : 3 * width],
            (((0,), (0,)), ((), ())),
            precision=lax.Precision.HIGHEST,
            preferred_element_type=jnp.float32,
        ) * (LEN ** -0.5)
        for peer in range(n):
            for m in range(3):
                first = m * width + peer * rows
                pieces[peer, m] = product[first : first + rows, m * width : (m + 1) * width]
        to_others(lambda copy: copy.start())
        shared[lane, mine] = pieces[me]

    for b in range(groups):
        for example, end in enumerate((0, last)):
            @pl.when(jnp.logical_not((lane == b) & (me == end)))
            def _(b=b, example=example, end=end):
                pltpu.make_async_remote_copy(
                    src_ref=pieces.at[0],
                    dst_ref=shared.at[b, example],
                    send_sem=spread_send.at[0, 0],
                    recv_sem=spread_recv.at[b, example],
                    device_id={"dp": b, "tensor": end},
                    device_id_type=MESH,
                ).wait_recv()

    out[...] = shared[...]

    @pl.when(at_end)
    def _():
        to_others(lambda copy: copy.wait_send())

    for chunk in range(CHUNKS):
        for piece in range(PIECES):
            @pl.when(me > 0)
            def _(chunk=chunk, piece=piece):
                send(0, chunk, piece).wait_send()

            @pl.when(me < last)
            def _(chunk=chunk, piece=piece):
                send(1, chunk, piece).wait_send()


def score_kernel(n, groups, examples, terms, out, blocks, arrived, send_sem, recv_sem):
    me, lane = lax.axis_index("tensor"), lax.axis_index("dp")
    split = n // groups
    columns = out.shape[1]
    source = me // split
    own = lane == source

    barrier = pltpu.get_barrier_semaphore()
    for t in range(n):
        @pl.when(jnp.logical_not(own & (me == t)))
        def _(t=t):
            pl.semaphore_signal(barrier, inc=1, device_id={"dp": source, "tensor": t}, device_id_type=MESH)

    for b in range(groups):
        for s in range(split):
            blocks[b * split + s] = (
                terms[b * examples : (b + 1) * examples, s * columns : (s + 1) * columns]
                + terms[
                    (groups + b) * examples : (groups + b + 1) * examples,
                    s * columns : (s + 1) * columns,
                ]
            )

    @pl.when(own)
    def _():
        pl.semaphore_wait(barrier, n - 1)

    @pl.when(jnp.logical_not(own))
    def _():
        pl.semaphore_wait(barrier, n)

    def send(b, s):
        return pltpu.make_async_remote_copy(
            src_ref=blocks.at[b * split + s],
            dst_ref=arrived.at[me],
            send_sem=send_sem.at[b * split + s],
            recv_sem=recv_sem.at[me],
            device_id={"dp": b, "tensor": lane * split + s},
            device_id_type=MESH,
        )

    def to_me(b, s):
        return (lane == b) & (me == lane * split + s)

    for b in range(groups):
        for s in range(split):
            @pl.when(jnp.logical_not(to_me(b, s)))
            def _(b=b, s=s):
                send(b, s).start()

            @pl.when(to_me(b, s))
            def _(b=b, s=s):
                arrived[me] = blocks[b * split + s]

    def wait_from(t):
        pltpu.make_async_remote_copy(
            src_ref=blocks.at[0],
            dst_ref=arrived.at[t],
            send_sem=send_sem.at[0],
            recv_sem=recv_sem.at[t],
            device_id={"dp": source, "tensor": t},
            device_id_type=MESH,
        ).wait_recv()

    for t in range(n):
        @pl.when(jnp.logical_not(own & (me == t)))
        def _(t=t):
            wait_from(t)

    total = arrived[0]
    for t in range(1, n):
        total = total + arrived[t]
    out[...] = total
    for b in range(groups):
        for s in range(split):
            @pl.when(jnp.logical_not(to_me(b, s)))
            def _(b=b, s=s):
                send(b, s).wait_send()


def shards(n, groups, *arrays):
    values, factors, queries = arrays[:5], arrays[5:10], arrays[10]
    width = factors[1].shape[1]
    local = values[0].shape[0]
    examples, rows = local // LEN, width // n
    f32, bf16 = jnp.float32, jnp.bfloat16
    dma = pltpu.SemaphoreType.DMA
    turned = [factors[0]] + [w.T for w in factors[1:]]
    gradients = pl.pallas_call(
        functools.partial(gradient_kernel, n, groups, width),
        out_shape=jax.ShapeDtypeStruct((groups, examples, 3, rows, width), f32),
        in_specs=[pl.BlockSpec(memory_space=pl.ANY)] * 10,
        out_specs=pl.BlockSpec(memory_space=pltpu.VMEM),
        scratch_shapes=[pltpu.VMEM((CHUNKS, 2 * CHUNK, v.shape[1]), bf16) for v in values]
        + [pltpu.VMEM(w.shape, bf16) for w in turned]
        + [
            pltpu.VMEM((CHUNKS, 2 * CHUNK, 6 * width), f32),
            pltpu.VMEM((CHUNKS, 2 * CHUNK, 6 * width), f32),
            pltpu.VMEM((n, 3, rows, width), f32),
            pltpu.VMEM((groups, examples, 3, rows, width), f32),
            dma((CHUNKS, 5, 2)),
            dma((5,)),
            dma((2, CHUNKS, PIECES)),
            dma((2, CHUNKS, PIECES)),
            dma((groups, n)),
            dma((groups, examples)),
        ]
        + [pltpu.VMEM(w.shape, bf16) for w in factors[1:]],
        compiler_params=pltpu.CompilerParams(
            collective_id=0, has_side_effects=True, vmem_limit_bytes=56 * 2**20
        ),
    )(*values, *turned)
    gradients = gradients.reshape(groups * examples, 3, rows * width)
    high = lax.reduce_precision(gradients, 8, 7)
    low = gradients - high
    both = jnp.concatenate([high, low], 0).astype(bf16)
    terms = jnp.einsum("emv,qmv->eq", both, queries, preferred_element_type=f32)
    columns = terms.shape[1] * groups // n
    return pl.pallas_call(
        functools.partial(score_kernel, n, groups, examples),
        out_shape=jax.ShapeDtypeStruct((examples, columns), f32),
        in_specs=[pl.BlockSpec(memory_space=pltpu.VMEM)],
        out_specs=pl.BlockSpec(memory_space=pltpu.VMEM),
        scratch_shapes=[
            pltpu.VMEM((n, examples, columns), f32),
            pltpu.VMEM((n, examples, columns), f32),
            dma((n,)),
            dma((n,)),
        ],
        compiler_params=pltpu.CompilerParams(collective_id=1, has_side_effects=True),
    )(terms)


def solution(mesh):
    placed = (
        P(("parts", "dp"), "tensor"),
        P(("parts", "dp"), "tensor"),
        P(("parts", "dp"), "tensor"),
        P(("parts", "dp"), "tensor"),
        P(("parts", "dp"), "tensor"),
        P("tensor", None),
        P("tensor", None),
        P("tensor", None),
        P("tensor", None),
        P("tensor", None),
        P("dp", None, "tensor"),
    )
    return jax.shard_map(
        functools.partial(shards, mesh.shape["tensor"], mesh.shape["dp"]),
        mesh=mesh,
        in_specs=placed,
        out_specs=P(("parts", "dp"), "tensor"),
        check_vma=False,
    )
```

```python
import functools

import jax
import jax.numpy as jnp
from jax import lax
from jax.experimental import pallas as pl
from jax.experimental.pallas import tpu as pltpu
from jax.sharding import PartitionSpec as P

LEN = 512
MESH = pl.DeviceIdType.MESH
AHEAD = 1
CHUNKS = 4
CHUNK = LEN // CHUNKS
PIECES = 4
PIECE = CHUNK // PIECES


def gradient_kernel(n, groups, width, *refs):
    values, factors, out = refs[:5], refs[5:10], refs[10]
    held, weights = refs[11:16], refs[16:21]
    (terms, arrived, pieces, shared, load_sem, weight_sem,
     send_sem, recv_sem, spread_send, spread_recv) = refs[21:31]
    upright = refs[31:]
    me, lane = lax.axis_index("tensor"), lax.axis_index("dp")
    rows = width // n
    last = n - 1
    at_end = (me == 0) | (me == last)
    mine = jnp.where(me == 0, 0, 1)

    def load(step, k, example):
        start = pl.multiple_of(example * LEN + step * CHUNK, CHUNK)
        return pltpu.make_async_copy(
            values[k].at[pl.ds(start, CHUNK)],
            held[k].at[step, pl.ds(example * CHUNK, CHUNK)],
            load_sem.at[step, k, example],
        )

    def weight(k):
        return pltpu.make_async_copy(factors[k], weights[k], weight_sem.at[k])

    for step in range(AHEAD):
        for k in range(5):
            if step == 0:
                weight(k).start()
            load(step, k, 0).start()
            load(step, k, 1).start()

    barrier = pltpu.get_barrier_semaphore()

    def greet(there, target):
        @pl.when(there)
        def _():
            pl.semaphore_signal(barrier, inc=1, device_id=target, device_id_type=MESH)

    greet(me > 0, {"dp": lane, "tensor": jnp.maximum(me - 1, 0)})
    greet(me < last, {"dp": lane, "tensor": jnp.minimum(me + 1, last)})
    for b in range(groups):
        for end in (0, last):
            greet(jnp.logical_not((lane == b) & (me == end)), {"dp": b, "tensor": end})

    for k in range(5):
        weight(k).wait()
        if k:
            upright[k - 1][...] = weights[k][...].T

    @pl.when(at_end)
    def _():
        pl.semaphore_wait(barrier, n * groups)

    @pl.when(jnp.logical_not(at_end))
    def _():
        pl.semaphore_wait(barrier, 2)

    def send(example, chunk, piece):
        target = jnp.maximum(me - 1, 0) if example == 0 else jnp.minimum(me + 1, last)
        part = pl.ds(example * CHUNK + piece * PIECE, PIECE)
        return pltpu.make_async_remote_copy(
            src_ref=terms.at[chunk, part],
            dst_ref=arrived.at[chunk, part],
            send_sem=send_sem.at[example, chunk, piece],
            recv_sem=recv_sem.at[example, chunk, piece],
            device_id={"dp": lane, "tensor": target},
            device_id_type=MESH,
        )

    def advance(step, carry):
        @pl.when(step < CHUNKS)
        def _():
            column = 0
            for k in range(5):
                load(step, k, 0).wait()
                load(step, k, 1).wait()

                @pl.when(step + AHEAD < CHUNKS)
                def _(k=k):
                    load(step + AHEAD, k, 0).start()
                    load(step + AHEAD, k, 1).start()

                turned = 1 if k else 0
                share = weights[k].shape[1 - turned]
                terms[step, :, column : column + share] = lax.dot_general(
                    held[k][step],
                    upright[k - 1][...] if k else weights[k][...],
                    (((1,), (0,)), ((), ())),
                    preferred_element_type=jnp.float32,
                )
                column += share

        for piece in range(PIECES):
            for example in range(2):
                hops = last - me if example == 0 else me
                chunk = step - hops
                first = example * CHUNK + piece * PIECE
                part = slice(first, first + PIECE)
                active = (chunk >= 0) & (chunk < CHUNKS)

                @pl.when(active & (hops > 0))
                def _(example=example, chunk=chunk, piece=piece, part=part):
                    send(example, chunk, piece).wait_recv()
                    terms[chunk, part, :] = terms[chunk, part, :] + arrived[chunk, part, :]

                @pl.when(active & (hops < last))
                def _(example=example, chunk=chunk, piece=piece):
                    send(example, chunk, piece).start()

        return carry

    lax.fori_loop(0, CHUNKS + last, advance, 0)

    def spread(b, peer):
        return pltpu.make_async_remote_copy(
            src_ref=pieces.at[peer],
            dst_ref=shared.at[lane, mine],
            send_sem=spread_send.at[b, peer],
            recv_sem=spread_recv.at[lane, mine],
            device_id={"dp": b, "tensor": peer},
            device_id_type=MESH,
        )

    def to_others(action):
        def visit(q, carry):
            b, peer = q // n, lax.rem(q, n)

            @pl.when(jnp.logical_not((b == lane) & (peer == me)))
            def _():
                action(spread(b, peer))

            return carry

        lax.fori_loop(0, groups * n, visit, 0)

    @pl.when(at_end)
    def _():
        start = pl.multiple_of(mine * CHUNK, CHUNK)
        total = terms[:, pl.ds(start, CHUNK), :].reshape(LEN, 6 * width)
        product = lax.dot_general(
            total[:, 3 * width :],
            total[:, : 3 * width],
            (((0,), (0,)), ((), ())),
            precision=lax.Precision.HIGHEST,
            preferred_element_type=jnp.float32,
        ) * (LEN ** -0.5)
        for peer in range(n):
            for m in range(3):
                first = m * width + peer * rows
                pieces[peer, m] = product[first : first + rows, m * width : (m + 1) * width]
        to_others(lambda copy: copy.start())
        shared[lane, mine] = pieces[me]

    for b in range(groups):
        for example, end in enumerate((0, last)):
            @pl.when(jnp.logical_not((lane == b) & (me == end)))
            def _(b=b, example=example, end=end):
                pltpu.make_async_remote_copy(
                    src_ref=pieces.at[0],
                    dst_ref=shared.at[b, example],
                    send_sem=spread_send.at[0, 0],
                    recv_sem=spread_recv.at[b, example],
                    device_id={"dp": b, "tensor": end},
                    device_id_type=MESH,
                ).wait_recv()

    out[...] = shared[...]

    @pl.when(at_end)
    def _():
        to_others(lambda copy: copy.wait_send())

    for chunk in range(CHUNKS):
        for piece in range(PIECES):
            @pl.when(me > 0)
            def _(chunk=chunk, piece=piece):
                send(0, chunk, piece).wait_send()

            @pl.when(me < last)
            def _(chunk=chunk, piece=piece):
                send(1, chunk, piece).wait_send()


def score_kernel(n, groups, examples, terms, out, blocks, arrived, send_sem, recv_sem):
    me, lane = lax.axis_index("tensor"), lax.axis_index("dp")
    split = n // groups
    columns = out.shape[1]
    source = me // split
    own = lane == source

    barrier = pltpu.get_barrier_semaphore()
    for t in range(n):
        @pl.when(jnp.logical_not(own & (me == t)))
        def _(t=t):
            pl.semaphore_signal(barrier, inc=1, device_id={"dp": source, "tensor": t}, device_id_type=MESH)

    for b in range(groups):
        for s in range(split):
            blocks[b * split + s] = (
                terms[b * examples : (b + 1) * examples, s * columns : (s + 1) * columns]
                + terms[
                    (groups + b) * examples : (groups + b + 1) * examples,
                    s * columns : (s + 1) * columns,
                ]
            )

    @pl.when(own)
    def _():
        pl.semaphore_wait(barrier, n - 1)

    @pl.when(jnp.logical_not(own))
    def _():
        pl.semaphore_wait(barrier, n)

    def send(b, s):
        return pltpu.make_async_remote_copy(
            src_ref=blocks.at[b * split + s],
            dst_ref=arrived.at[me],
            send_sem=send_sem.at[b * split + s],
            recv_sem=recv_sem.at[me],
            device_id={"dp": b, "tensor": lane * split + s},
            device_id_type=MESH,
        )

    def to_me(b, s):
        return (lane == b) & (me == lane * split + s)

    for b in range(groups):
        for s in range(split):
            @pl.when(jnp.logical_not(to_me(b, s)))
            def _(b=b, s=s):
                send(b, s).start()

            @pl.when(to_me(b, s))
            def _(b=b, s=s):
                arrived[me] = blocks[b * split + s]

    def wait_from(t):
        pltpu.make_async_remote_copy(
            src_ref=blocks.at[0],
            dst_ref=arrived.at[t],
            send_sem=send_sem.at[0],
            recv_sem=recv_sem.at[t],
            device_id={"dp": source, "tensor": t},
            device_id_type=MESH,
        ).wait_recv()

    for t in range(n):
        @pl.when(jnp.logical_not(own & (me == t)))
        def _(t=t):
            wait_from(t)

    total = arrived[0]
    for t in range(1, n):
        total = total + arrived[t]
    out[...] = total
    for b in range(groups):
        for s in range(split):
            @pl.when(jnp.logical_not(to_me(b, s)))
            def _(b=b, s=s):
                send(b, s).wait_send()


def shards(n, groups, *arrays):
    values, factors, queries = arrays[:5], arrays[5:10], arrays[10]
    width = factors[1].shape[1]
    local = values[0].shape[0]
    examples, rows = local // LEN, width // n
    f32, bf16 = jnp.float32, jnp.bfloat16
    dma = pltpu.SemaphoreType.DMA
    turned = [factors[0]] + [w.T for w in factors[1:]]
    gradients = pl.pallas_call(
        functools.partial(gradient_kernel, n, groups, width),
        out_shape=jax.ShapeDtypeStruct((groups, examples, 3, rows, width), f32),
        in_specs=[pl.BlockSpec(memory_space=pl.ANY)] * 10,
        out_specs=pl.BlockSpec(memory_space=pltpu.VMEM),
        scratch_shapes=[pltpu.VMEM((CHUNKS, 2 * CHUNK, v.shape[1]), bf16) for v in values]
        + [pltpu.VMEM(w.shape, bf16) for w in turned]
        + [
            pltpu.VMEM((CHUNKS, 2 * CHUNK, 6 * width), f32),
            pltpu.VMEM((CHUNKS, 2 * CHUNK, 6 * width), f32),
            pltpu.VMEM((n, 3, rows, width), f32),
            pltpu.VMEM((groups, examples, 3, rows, width), f32),
            dma((CHUNKS, 5, 2)),
            dma((5,)),
            dma((2, CHUNKS, PIECES)),
            dma((2, CHUNKS, PIECES)),
            dma((groups, n)),
            dma((groups, examples)),
        ]
        + [pltpu.VMEM(w.shape, bf16) for w in factors[1:]],
        compiler_params=pltpu.CompilerParams(
            collective_id=0, has_side_effects=True, vmem_limit_bytes=56 * 2**20
        ),
    )(*values, *turned)
    gradients = gradients.reshape(groups * examples, 3, rows * width)
    high = lax.reduce_precision(gradients, 8, 7)
    low = gradients - high
    both = jnp.concatenate([high, low], 0).astype(bf16)
    terms = jnp.einsum("emv,qmv->eq", both, queries, preferred_element_type=f32)
    columns = terms.shape[1] * groups // n
    return pl.pallas_call(
        functools.partial(score_kernel, n, groups, examples),
        out_shape=jax.ShapeDtypeStruct((examples, columns), f32),
        in_specs=[pl.BlockSpec(memory_space=pltpu.VMEM)],
        out_specs=pl.BlockSpec(memory_space=pltpu.VMEM),
        scratch_shapes=[
            pltpu.VMEM((n, examples, columns), f32),
            pltpu.VMEM((n, examples, columns), f32),
            dma((n,)),
            dma((n,)),
        ],
        compiler_params=pltpu.CompilerParams(collective_id=1, has_side_effects=True),
    )(terms)


def solution(mesh):
    placed = (
        P(("parts", "dp"), "tensor"),
        P(("parts", "dp"), "tensor"),
        P(("parts", "dp"), "tensor"),
        P(("parts", "dp"), "tensor"),
        P(("parts", "dp"), "tensor"),
        P("tensor", None),
        P("tensor", None),
        P("tensor", None),
        P("tensor", None),
        P("tensor", None),
        P("dp", None, "tensor"),
    )
    return jax.shard_map(
        functools.partial(shards, mesh.shape["tensor"], mesh.shape["dp"]),
        mesh=mesh,
        in_specs=placed,
        out_specs=P(("parts", "dp"), "tensor"),
        check_vma=False,
    )
```
